32 devices in a mesh: panel: 8 (over y, x, core), slab: 4 (over z).
Axes of the slice: x: 2, y: 2, z: 4, core: 2. Of those that a mesh axis runs over, the one named last changes fastest.
Arguments:
- clip_cache: float32 [1024, 1024], P(None, 'panel'), may hold values from -6 to 6
- dose_scale: float32 [16, 1024], P(None, 'panel'), may hold values from 0.3 to 3
- focus_term: float32 [8, 1024], P(None, 'panel'), may hold values from -3 to 3
- clip_ids: int32 [32768], P('slab'), may hold values from 0 to 1023
- dose_ids: int32 [32768], P('slab'), may hold values from 0 to 15
- focus_ids: int32 [32768], P('slab'), may hold values from 0 to 7
Outputs:
- rotated: float32 [32768, 1024], P('slab', 'panel')
The draws below stay inside these ranges and needn't reach their ends.
All inputs are finite; a program needn't handle non-finite values.
Results may differ from the reference program's by a relative error of at most 0.0001.
Values sent between devices are 32-bit elements; how exact they have to be, the bound alone decides.
No kernel may reach another device: no remote copies, remote signals or barrier semaphores. Data moves between devices by JAX's collectives and lax.ppermute only.
A program may use at most 64 MiB of HBM per device.

```python
import math
import jax
import jax.numpy as jnp
from jax import lax

PANEL_COLS = 128
ROUNDS = 2
NCLIP = 1024
NDOSE = 16
NFOCUS = 8
M = 32768
NCOL = 1024
N_PANEL = 8


def plant(values, own_key, low, largest):
    place = [jax.random.randint(jax.random.fold_in(own_key, axis), (), 0, length) for axis, length in enumerate(values.shape)]
    longest = values.shape.index(max(values.shape))
    neighbour = place[:longest] + [(place[longest] + 1) % values.shape[longest]] + place[longest + 1:]
    return values.at[tuple(place)].set(low).at[tuple(neighbour)].set(largest)


def steps_of(stream_key, dims, cuts, least, top_value):
    def one(position, blocks):
        heights = jax.random.uniform(jax.random.fold_in(jax.random.fold_in(stream_key, 6), position), (blocks,), jnp.float32, least / len(cuts), top_value / len(cuts))
        return jnp.repeat(jnp.exp(heights), dims[position] // blocks).reshape((-1,) + (1,) * (len(dims) - position - 1))

    gain = one(*cuts[0])
    for cut in cuts[1:]:
        gain = gain * one(*cut)
    return gain


def normal_values(key, extent, scale, bound, cuts=(), kind=jnp.bfloat16):
    entries = scale * jax.random.normal(key, extent, jnp.float32)
    if cuts:
        entries = entries * steps_of(key, extent, cuts, -0.22, 0.18)
    return jnp.clip(entries, -bound, bound).astype(kind)


def setup_inputs(seed: int = 0) -> dict:
    splits = jax.random.split(jax.random.key(seed), 7)
    clip_cache = normal_values(splits[0], (NCLIP, NCOL), 1.0, 6.0, ((1, 8),), jnp.float32)
    dose_scale = jnp.clip(jnp.exp(math.log(3.0) - 2.3025851 * jax.random.uniform(splits[1], (NDOSE, NCOL), jnp.float32) ** steps_of(splits[1], (NDOSE, NCOL), ((1, 8),), -0.2, 0.2)), 0.3, 3.0)
    focus_term = normal_values(splits[2], (NFOCUS, NCOL), 0.5, 3.0, ((1, 8),), jnp.float32)
    clip_ids = plant(jax.random.randint(splits[3], (M,), 0, NCLIP), jax.random.fold_in(splits[3], 1), 0, NCLIP - 1).astype(jnp.int32)
    dose_ids = plant(jax.random.randint(splits[4], (M,), 0, NDOSE), jax.random.fold_in(splits[4], 1), 0, NDOSE - 1).astype(jnp.int32)
    focus_ids = plant(jax.random.randint(splits[5], (M,), 0, NFOCUS), jax.random.fold_in(splits[5], 1), 0, NFOCUS - 1).astype(jnp.int32)
    return dict(clip_cache=clip_cache, dose_scale=dose_scale, focus_term=focus_term, clip_ids=clip_ids, dose_ids=dose_ids, focus_ids=focus_ids)


EPSILON = 1e-06

def block_rotation(gram):
    doubled = gram.shape[0]
    half_size = doubled // 2
    diagonal = jnp.diagonal(gram)
    coupling = gram / (diagonal[:, None] + diagonal[None, :])
    positions = lax.iota(jnp.int32, doubled)
    upper_mask = (positions[:, None] < half_size) & (positions[None, :] >= half_size)
    lower_mask = (positions[:, None] >= half_size) & (positions[None, :] < half_size)
    generator = 0.5 * (jnp.where(upper_mask, coupling, 0.0) - jnp.where(lower_mask, coupling, 0.0))
    identity = jnp.eye(doubled, dtype=gram.dtype)
    plus_half = identity + generator
    symmetric = identity + jnp.dot(generator.T.astype(jnp.float32), generator.astype(jnp.float32), precision=lax.Precision.HIGHEST, preferred_element_type=jnp.float32)
    factor = jnp.linalg.cholesky(symmetric)
    numerator = jnp.dot(plus_half.astype(jnp.float32), plus_half.astype(jnp.float32), precision=lax.Precision.HIGHEST, preferred_element_type=jnp.float32)
    return jax.scipy.linalg.cho_solve((factor, True), numerator)

def rotate_pair(pair):
    left_panel, right_panel = pair
    panel_width = left_panel.shape[1]
    pair_block = jnp.concatenate([left_panel, right_panel], axis=1)
    gram = lax.dot_general(pair_block.astype(jnp.float32), pair_block.astype(jnp.float32), (((0,), (0,)), ((), ())), precision=lax.Precision.HIGHEST, preferred_element_type=jnp.float32)
    rotated = jnp.dot(pair_block.astype(jnp.float32), block_rotation(gram).astype(jnp.float32), precision=lax.Precision.HIGHEST, preferred_element_type=jnp.float32)
    return (rotated[:, :panel_width], rotated[:, panel_width:])

def reference(clip_cache, dose_scale, focus_term, clip_ids, dose_ids, focus_ids):
    jacobian = clip_cache[clip_ids] * dose_scale[dose_ids] + focus_term[focus_ids]
    col_squares = lax.optimization_barrier(jnp.sum(jacobian * jacobian, axis=0))
    jacobian = jacobian * (1.0 / jnp.sqrt(col_squares / M + EPSILON))
    panels = jacobian.reshape(M, N_PANEL, PANEL_COLS).transpose(1, 0, 2)
    evens = panels[0::2]
    odds = panels[1::2]
    for section in range(ROUNDS):
        if section > 0:
            seats = jnp.stack([evens, odds], axis=1).reshape(N_PANEL, M, PANEL_COLS)
            seats = jnp.roll(seats, 1, axis=0)
            evens = seats[0::2]
            odds = seats[1::2]
        evens, odds = lax.map(rotate_pair, (evens, odds))
    seats = jnp.stack([evens, odds], axis=1).reshape(N_PANEL, M, PANEL_COLS)
    return seats.transpose(1, 0, 2).reshape(M, N_PANEL * PANEL_COLS)
```

```python
import jax
import jax.numpy as jnp
from jax import lax
from jax.experimental import pallas as pl
from jax.experimental.pallas import tpu as pltpu
from jax.sharding import PartitionSpec as P

EPSILON = 1e-06
VMEM_LIMIT = 48 * 2**20
HIGHEST = lax.Precision.HIGHEST
COUNT_PARTS = 2
MARGIN = 8
BRIEF = pl.CostEstimate(flops=1, bytes_accessed=1, transcendentals=0)


def from_partner(value):
    count = lax.axis_size("panel")
    return lax.ppermute(value, "panel", [(i, i ^ 1) for i in range(count)])


def from_previous_pair(value):
    count = lax.axis_size("panel")
    return lax.ppermute(value, "panel", [(i, (i + 2) % count) for i in range(count)])


def from_other_slabs(value):
    slabs = lax.axis_size("slab")
    paired = slabs & (slabs - 1) == 0
    target = lambda i, d: i ^ d if paired else (i + d) % slabs
    return [
        lax.ppermute(value, "slab", [(i, target(i, d)) for i in range(slabs)])
        for d in range(1, slabs)
    ]


def split(value):
    high = value.astype(jnp.bfloat16)
    low = (value - high.astype(jnp.float32)).astype(jnp.bfloat16)
    return high, low


def bdot(left, right, dims=((1,), (0,))):
    return lax.dot_general(left, right, (dims, ((), ())), preferred_element_type=jnp.float32)


def split3(value):
    high, rest = split(value)
    middle = value - high.astype(jnp.float32)
    low = (middle - rest.astype(jnp.float32)).astype(jnp.bfloat16)
    return high, rest, low


def dot3(left, right):
    (a, b), (c, d) = split(left), split(right)
    return bdot(jnp.concatenate([a, b, a], axis=1), jnp.concatenate([c, c, d], axis=0))


def dot6(left, right):
    (a, b, c), (d, e, f) = split3(left), split3(right)
    lefts, rights = [a, a, b, b, a, c], [d, e, d, e, f, d]
    return bdot(jnp.concatenate(lefts, axis=1), jnp.concatenate(rights, axis=0))


def fdot(left, right, dims=((1,), (0,))):
    return lax.dot_general(
        left, right, (dims, ((), ())), precision=HIGHEST, preferred_element_type=jnp.float32
    )


def layout_kernel(odd_ref, clips, doses, focuses, *refs):
    id_refs, (table, ids, own, pairs), spaces, sems = refs[:3], refs[3:7], refs[7:10], refs[10]
    start = 0
    copies = []
    for k, ref in enumerate((clips, doses, focuses)):
        part = table.at[pl.ds(start, ref.shape[0])]
        copies.append(pltpu.make_async_copy(ref, part, sems.at[k]))
        start += ref.shape[0]
    for k, (ref, space) in enumerate(zip(id_refs, spaces)):
        copies.append(pltpu.make_async_copy(ref, space, sems.at[3 + k]))
    for copy in copies:
        copy.start()
    half = own.shape[1]
    begin = pl.multiple_of(odd_ref[0] * half, half)
    for k, space in enumerate(spaces):
        copies[3 + k].wait()
        ids[k : k + 1, :] = space[...]
        own[k : k + 1, :] = space[:, pl.ds(begin, half)]
    pairs[...] = ids[1:2, :] * clips.shape[0] + ids[0:1, :]
    for copy in copies[:3]:
        copy.wait()


def layout(odd, clip_cache, dose_scale, focus_term, *ids):
    rows = clip_cache.shape[0] + dose_scale.shape[0] + focus_term.shape[0]
    count = ids[0].shape[0]
    return pl.pallas_call(
        layout_kernel,
        in_specs=[pl.BlockSpec(memory_space=pltpu.SMEM)]
        + [pl.BlockSpec(memory_space=pltpu.HBM)] * 6,
        out_shape=(
            jax.ShapeDtypeStruct((rows, clip_cache.shape[1]), jnp.float32),
            jax.ShapeDtypeStruct((len(ids), count), jnp.int32),
            jax.ShapeDtypeStruct((len(ids), count // 2), jnp.int32),
            jax.ShapeDtypeStruct((1, count), jnp.int32),
        ),
        scratch_shapes=[pltpu.VMEM((1, count), jnp.int32)] * 3 + [pltpu.SemaphoreType.DMA((6,))],
        compiler_params=pltpu.CompilerParams(vmem_limit_bytes=60 * 2**20),
        cost_estimate=BRIEF,
        name="layout",
    )(odd, clip_cache, dose_scale, focus_term, *[value.reshape(1, count) for value in ids])


def one_hot(index, first, size):
    positions = first + lax.broadcasted_iota(jnp.int32, (size, index.shape[1]), 0)
    return jnp.where(positions == index, 1.0, 0.0).astype(jnp.bfloat16)


def first_counts_kernel(focus_count, table, ids, *refs):
    outs, copied, sem = refs[:COUNT_PARTS], refs[COUNT_PARTS], refs[COUNT_PARTS + 1]
    copy = pltpu.make_async_copy(table, copied, sem)
    copy.start()
    counts_kernel(focus_count, 0, ids, *outs)
    copy.wait()


def first_counts_of(table, ids, clip_count, dose_count, focus_count):
    settings = dose_count * focus_count
    part = jax.ShapeDtypeStruct((settings // COUNT_PARTS, clip_count), jnp.float32)
    return pl.pallas_call(
        lambda *refs: first_counts_kernel(focus_count, *refs),
        in_specs=[pl.BlockSpec(memory_space=pltpu.HBM), pl.BlockSpec(memory_space=pltpu.VMEM)],
        out_shape=[part] * COUNT_PARTS + [jax.ShapeDtypeStruct(table.shape, table.dtype)],
        scratch_shapes=[pltpu.SemaphoreType.DMA],
        compiler_params=pltpu.CompilerParams(vmem_limit_bytes=VMEM_LIMIT),
        cost_estimate=BRIEF,
        name="counts",
    )(table, ids)


def counts_kernel(focus_count, given, *refs):
    count_refs, id_refs, outs = refs[:given], refs[given : -COUNT_PARTS], refs[-COUNT_PARTS:]
    part, clip_count = outs[0].shape
    settings = part * COUNT_PARTS
    half = clip_count // 2
    chunk = min(2048, id_refs[-1].shape[1])
    total = jnp.zeros((2 * settings, half), jnp.float32)
    for ids in id_refs:
        for start in range(0, ids.shape[1], chunk):
            some = slice(start, start + chunk)
            clip = ids[0:1, some]
            setting = ids[1:2, some] * focus_count + ids[2:3, some]
            upper = clip >= half
            left = one_hot(jnp.where(upper, setting + settings, setting), 0, 2 * settings)
            right = one_hot(jnp.where(upper, clip - half, clip), 0, half)
            total += bdot(left, right, ((1,), (1,)))
    for k, out in enumerate(outs):
        lower = total[k * part : (k + 1) * part]
        upper = total[settings + k * part : settings + (k + 1) * part]
        value = jnp.concatenate([lower, upper], axis=1)
        out[...] = count_refs[k][...] + value if given else value


def counts_of(ids, base, clip_count, dose_count, focus_count):
    settings = dose_count * focus_count
    part = jax.ShapeDtypeStruct((settings // COUNT_PARTS, clip_count), jnp.float32)
    return pl.pallas_call(
        lambda *refs: counts_kernel(focus_count, len(base), *refs),
        out_shape=[part] * COUNT_PARTS,
        compiler_params=pltpu.CompilerParams(vmem_limit_bytes=VMEM_LIMIT),
        cost_estimate=BRIEF,
        name="counts",
    )(*base, *ids)


def prepare_gram(counts, tables, sizes, out, high, low, doses, numbers):
    clip_count, dose_count, focus_count = sizes
    width = out.shape[0]
    panels = len(tables)
    for q, table in enumerate(tables):
        part = slice(q * width, (q + 1) * width)
        high[:, part], low[:, part] = split(table[:clip_count, :])
        doses[:, part] = table[clip_count : clip_count + dose_count, :]
    focuses = jnp.concatenate([table[clip_count + dose_count :, :] for table in tables], axis=1)

    counts_high, counts_low = split(counts)
    totals = (
        bdot(counts_high, high[...]) + bdot(counts_high, low[...]) + bdot(counts_low, high[...])
    )
    mixed = jnp.zeros((focus_count, panels * width), jnp.float32)
    per_focus = jnp.sum(counts, axis=1, keepdims=True)
    number = jnp.zeros((focus_count, 1), jnp.float32)
    for b in range(dose_count):
        some = slice(b * focus_count, (b + 1) * focus_count)
        mixed += totals[some] * doses[b : b + 1, :]
        number += per_focus[some]
        numbers[b : b + 1, :] = jnp.sum(counts[some], axis=0, keepdims=True)
    lefts = jnp.concatenate([focuses[:, :width], mixed[:, :width]], axis=0)
    rights = jnp.concatenate([mixed + number * focuses, focuses], axis=0)
    out[...] = fdot(lefts, rights, ((0,), (0,)))


def add_doses(first, own_doses, begin, group, columns, out, high, low, doses, numbers):
    width = out.shape[0]
    pieces = [first * numbers[pl.ds(begin + k, 1), :] for k in range(group)]
    left_high, left_low = split(jnp.concatenate(pieces, axis=0))
    products = (
        bdot(left_high, high[:, columns])
        + bdot(left_high, low[:, columns])
        + bdot(left_low, high[:, columns])
    )
    lanes = lax.broadcasted_iota(jnp.int32, own_doses.shape, 1)
    total = jnp.zeros_like(out[:, columns])
    for k in range(group):
        column = jnp.sum(jnp.where(lanes == begin + k, own_doses, 0.0), axis=1, keepdims=True)
        row = doses[pl.ds(begin + k, 1), columns]
        total += products[k * width : (k + 1) * width] * column * row
    out[:, columns] += total


def gram_scratch(clip_count, dose_count, total):
    return [
        pltpu.VMEM((clip_count, total), jnp.bfloat16),
        pltpu.VMEM((clip_count, total), jnp.bfloat16),
        pltpu.VMEM((dose_count, total), jnp.float32),
        pltpu.VMEM((dose_count, clip_count), jnp.float32),
    ]


def counts_from(refs):
    own, more = refs[:COUNT_PARTS], refs[COUNT_PARTS:]
    return jnp.concatenate([a[...] + b[...] for a, b in zip(own, more)], axis=0)


def pair_kernel(sizes, *refs):
    counts, refs = refs[: 2 * COUNT_PARTS], refs[2 * COUNT_PARTS :]
    own, partner, out, scratch = refs[0], refs[1], refs[2], refs[3:]
    clip_count, dose_count, _ = sizes
    prepare_gram(counts_from(counts), [own, partner], sizes, out, *scratch)
    first = own[:clip_count, :].T
    own_doses = own[clip_count : clip_count + dose_count, :].T
    group = 8

    def some_doses(step, carry):
        add_doses(first, own_doses, step * group, group, slice(None), out, *scratch)
        return carry

    lax.fori_loop(0, dose_count // group, some_doses, 0)


def pair_gram_of(counts, more, tables, sizes):
    width = tables[0].shape[1]
    return pl.pallas_call(
        lambda *refs: pair_kernel(sizes, *refs),
        out_shape=jax.ShapeDtypeStruct((width, 2 * width), jnp.float32),
        scratch_shapes=gram_scratch(*sizes[:2], 2 * width),
        compiler_params=pltpu.CompilerParams(vmem_limit_bytes=VMEM_LIMIT),
        cost_estimate=BRIEF,
        name="pair_gram",
    )(*counts, *more, *tables)


def quad_kernel(sizes, *refs):
    counts, refs = refs[: 2 * COUNT_PARTS], refs[2 * COUNT_PARTS :]
    tables, earlier, (out, sent, *laid_out) = refs[:4], refs[4], refs[5:]
    clip_count, dose_count, _ = sizes
    width = out.shape[0]
    prepare_gram(counts_from(counts), tables, sizes, out, *laid_out)
    first = tables[0][:clip_count, :].T
    own_doses = tables[0][clip_count : clip_count + dose_count, :].T
    group = 8

    def some_doses(step, carry):
        add_doses(first, own_doses, step * group, group, slice(None), out, *laid_out)
        return carry

    lax.fori_loop(0, dose_count // group, some_doses, 0)
    sent[:, :width] = earlier[:, :width]
    sent[:, width:] = out[:, : 3 * width]


def quad_gram_of(counts, more, tables, earlier, sizes):
    width = tables[0].shape[1]
    clip_count, dose_count, _ = sizes
    square = jax.ShapeDtypeStruct((width, 4 * width), jnp.float32)
    half = jax.ShapeDtypeStruct((clip_count, 4 * width), jnp.bfloat16)
    doses = jax.ShapeDtypeStruct((dose_count, 4 * width), jnp.float32)
    return pl.pallas_call(
        lambda *refs: quad_kernel(sizes, *refs),
        out_shape=(square, square, half, half, doses),
        scratch_shapes=gram_scratch(clip_count, dose_count, 4 * width)[3:],
        compiler_params=pltpu.CompilerParams(vmem_limit_bytes=VMEM_LIMIT),
        cost_estimate=BRIEF,
        name="quad_gram",
    )(*counts, *more, *tables, earlier)


def eye(size):
    rows = lax.broadcasted_iota(jnp.int32, (size, size), 0)
    cols = lax.broadcasted_iota(jnp.int32, (size, size), 1)
    return rows == cols


def diagonal_row(square):
    return jnp.sum(jnp.where(eye(square.shape[0]), square, 0.0), axis=0, keepdims=True)


def column_of(row):
    square = jnp.broadcast_to(row, (row.shape[1], row.shape[1]))
    return jnp.sum(jnp.where(eye(row.shape[1]), square, 0.0), axis=1, keepdims=True)


def inverses(couplings, factors, powers):
    products = [dot6(k, k.T) for k in couplings]
    bound = 0.0
    for product in products:
        rows = jnp.max(jnp.sum(jnp.abs(product), axis=0))
        frobenius = jnp.sqrt(jnp.max(jnp.sum(jnp.sum(product * product, axis=0, keepdims=True), axis=1)))
        bound = jnp.maximum(bound, jnp.minimum(rows, frobenius))
    size = products[0].shape[0]
    identity = jnp.where(eye(size), 1.0, 0.0)
    matrices = [identity + product for product in products]
    start = 2.0 / (2.0 + bound)
    rate = bound / (2.0 + bound)
    for factor, power, matrix in zip(factors, powers, matrices):
        error = identity - start * matrix
        factor[...] = identity + error
        power[...] = dot3(error, error)

    def square(rate):
        for factor, power in zip(factors, powers):
            value, now = power[...], factor[...]
            both = dot3(jnp.concatenate([now, value], axis=0), value)
            factor[...] = now + both[:size]
            power[...] = both[size:]
        return rate * rate

    lax.while_loop(lambda rate: rate > 3e-4, square, rate * rate)
    for factor in factors:
        factor[...] = start * factor[...]

    def correct(step, carry):
        for factor, matrix in zip(factors, matrices):
            guess = factor[...]
            factor[...] = guess + dot3(guess, identity - dot6(matrix, guess))
        return carry

    lax.fori_loop(0, jnp.where(bound > 4.0, 4, 1), correct, 0)
    return [factor[...] for factor in factors]


def weights_kernel(total_rows, odd_ref, pair_ref, own_ref, other_ref, weights, *spaces):
    width = weights.shape[0]
    odd = odd_ref[0] == 1
    sign = jnp.where(odd, -1.0, 1.0).astype(jnp.float32)
    block = lambda ref, j: ref[:, j * width : (j + 1) * width]
    identity = jnp.where(eye(width), 1.0, 0.0)

    diagonals = [
        diagonal_row(block(own_ref, 0)),
        diagonal_row(block(pair_ref, 0)),
        diagonal_row(block(other_ref, 1)),
        diagonal_row(block(other_ref, 0)),
    ]
    scales = [1.0 / jnp.sqrt(d / total_rows + EPSILON) for d in diagonals]
    columns = [column_of(s) for s in scales]
    scaled = lambda value, i, j: value * columns[i] * scales[j]
    squares = [d * s * s for d, s in zip(diagonals, scales)]

    own_a = scaled(block(own_ref, 0), 0, 0)
    own_b = scaled(block(pair_ref, 0), 1, 1)
    other_a = scaled(block(other_ref, 1), 2, 2)
    other_b = scaled(block(other_ref, 0), 3, 3)
    pair_a = scaled(block(own_ref, 3), 0, 2)
    pair_b = scaled(block(pair_ref, 1), 1, 3)
    cross_oo = scaled(block(own_ref, 1), 0, 1)
    cross_op = scaled(block(own_ref, 2), 0, 3)
    cross_po = scaled(block(other_ref, 3), 2, 1)
    cross_pp = scaled(block(other_ref, 2), 2, 3)

    coupling_a = sign * 0.5 * pair_a / (column_of(squares[0]) + squares[2])
    coupling_b = sign * 0.5 * pair_b / (column_of(squares[1]) + squares[3])
    inverse_a, inverse_b = inverses([coupling_a, coupling_b], spaces[:2], spaces[2:])

    def halves(inverse, coupling):
        own_partner = 2.0 * dot6(inverse, coupling)
        first = (2.0 * inverse - identity, -own_partner.T)
        second = (own_partner, identity - dot6(coupling.T, own_partner))
        return first, second

    own_cols_a, other_cols_a = halves(inverse_a, coupling_a)
    own_cols_b, other_cols_b = halves(inverse_b, coupling_b)
    left = [jnp.where(odd, o, p) for o, p in zip(own_cols_a, other_cols_a)]
    right = [jnp.where(odd, p, o) for o, p in zip(own_cols_b, other_cols_b)]
    left = jnp.concatenate(left, axis=0)
    right = jnp.concatenate(right, axis=0)

    def square_of(a, b, c):
        top = jnp.concatenate([a, b], axis=1)
        return jnp.concatenate([top, jnp.concatenate([b.T, c], axis=1)], axis=0)

    gram_a = square_of(own_a, pair_a, other_a)
    gram_b = square_of(own_b, pair_b, other_b)
    cross = jnp.concatenate(
        [
            jnp.concatenate([cross_oo, cross_op], axis=1),
            jnp.concatenate([cross_po, cross_pp], axis=1),
        ],
        axis=0,
    )
    left_squares = jnp.sum(left * dot3(gram_a, left), axis=0, keepdims=True)
    right_squares = jnp.sum(right * dot3(gram_b, right), axis=0, keepdims=True)
    between = dot3(left.T, dot3(cross, right))
    coupling = 0.5 * between / (column_of(left_squares) + right_squares)
    (inverse,) = inverses([coupling], spaces[:1], spaces[2:3])
    first, second = halves(inverse, coupling)
    top = jnp.where(odd, second[0], first[0])
    bottom = jnp.where(odd, second[1], first[1])
    part_a = dot6(left, top)
    part_b = dot6(right, bottom)
    for k, (part, half, column) in enumerate(
        [(part_a, 0, 0), (part_b, 0, 1), (part_b, 1, 3), (part_a, 1, 2)]
    ):
        piece = part[half * width : (half + 1) * width] * columns[column]
        weights[:, k * width : (k + 1) * width] = piece.T


def weights_of(odd, pair_gram, own_gram, other_gram, total_rows):
    width = own_gram.shape[0]
    whole = lambda value: pl.BlockSpec(value.shape, lambda: (0, 0))
    return pl.pallas_call(
        lambda *refs: weights_kernel(total_rows, *refs),
        in_specs=[pl.BlockSpec(memory_space=pltpu.SMEM)]
        + [whole(value) for value in (pair_gram, own_gram, other_gram)],
        out_specs=pl.BlockSpec((width, 4 * width), lambda: (0, 0)),
        out_shape=jax.ShapeDtypeStruct((width, 4 * width), jnp.float32),
        scratch_shapes=[pltpu.VMEM((width, width), jnp.float32)] * 4,
        compiler_params=pltpu.CompilerParams(vmem_limit_bytes=VMEM_LIMIT),
        name="weights",
    )(odd, pair_gram, own_gram, other_gram)


def rotate_kernel(group, piece, start, high, low, doses, weights, pairs, ids, *refs):
    tables, (out, products, left, places, rows, place_sem, out_sems) = refs[:4], refs[4:]
    clip_count, width = high.shape[0], weights.shape[0]
    over_lanes = ((1,), (1,))
    tall = MARGIN
    fetch = pltpu.make_async_copy(pairs, places, place_sem)
    fetch.start()
    focuses = jnp.concatenate([table[start:, :] for table in tables], axis=1)
    focus_count = focuses.shape[0]
    shifts = jnp.concatenate(split(fdot(focuses, weights[...], over_lanes)), axis=0)
    left[...] = jnp.concatenate([high[...], low[...], high[...]], axis=1)

    def some_doses(step, carry):
        scaled = [weights[...] * doses[pl.ds(step * group + k, 1), :] for k in range(group)]
        right_high, right_low = split(jnp.concatenate(scaled, axis=0))
        right = jnp.concatenate([right_high, right_high, right_low], axis=1)
        result = bdot(left[...], right, over_lanes)
        for k in range(group):
            begin = pl.multiple_of((step * group + k) * clip_count + tall, tall)
            products[pl.ds(begin, clip_count), :] = result[:, k * width : (k + 1) * width]
        return carry

    lax.fori_loop(0, doses.shape[0] // group, some_doses, 0)
    fetch.wait()
    unroll = 256
    sublanes = lax.broadcasted_iota(jnp.int32, (tall, width), 0)
    slots = lax.broadcasted_iota(jnp.int32, (2 * focus_count, unroll), 0)
    slots = jnp.where(slots >= focus_count, slots - focus_count, slots)

    def some_rows(part, carry):
        first = pl.multiple_of(part * unroll, unroll)
        hot = jnp.where(slots == ids[2:3, pl.ds(first, unroll)], 1.0, 0.0).astype(jnp.bfloat16)
        moved = bdot(hot, shifts, ((0,), (0,)))
        for begin in range(0, unroll, tall):
            starts = [places[0, first + begin + k] + (tall - k) for k in range(tall)]
            found = [products[pl.ds(start, tall), :] for start in starts]
            tile = found[0]
            for k in range(1, tall):
                tile = jnp.where(sublanes == k, found[k], tile)
            rows[pl.ds(first + begin, tall), :] = tile + moved[begin : begin + tall]
        return carry

    copies = []
    for k in range(rows.shape[0] // piece):
        lax.fori_loop(k * piece // unroll, (k + 1) * piece // unroll, some_rows, 0)
        span = pl.ds(k * piece, piece)
        copies.append(pltpu.make_async_copy(rows.at[span], out.at[span], out_sems.at[k]))
        copies[-1].start()
    for copy in copies:
        copy.wait()


def rotate(high, low, doses, weights, pairs, ids, tables, sizes):
    width = weights.shape[0]
    clip_count, dose_count, _ = sizes
    count = pairs.shape[1]
    piece = min(1024, count)
    vmem = pl.BlockSpec(memory_space=pltpu.VMEM)
    return pl.pallas_call(
        lambda *refs: rotate_kernel(8, piece, clip_count + dose_count, *refs),
        in_specs=[vmem] * 4 + [pl.BlockSpec(memory_space=pl.ANY)] + [vmem] * 5,
        out_specs=pl.BlockSpec(memory_space=pltpu.HBM),
        out_shape=jax.ShapeDtypeStruct((count, width), jnp.float32),
        scratch_shapes=[
            pltpu.VMEM((dose_count * clip_count + 2 * MARGIN, width), jnp.float32),
            pltpu.VMEM((clip_count, 3 * high.shape[1]), jnp.bfloat16),
            pltpu.SMEM((1, count), jnp.int32),
            pltpu.VMEM((count, width), jnp.float32),
            pltpu.SemaphoreType.DMA,
            pltpu.SemaphoreType.DMA((count // piece,)),
        ],
        compiler_params=pltpu.CompilerParams(vmem_limit_bytes=VMEM_LIMIT),
        name="rotate",
    )(high, low, doses, weights, pairs, ids, *tables)


def shards(clip_cache, dose_scale, focus_term, clip_ids, dose_ids, focus_ids):
    row_count = clip_ids.shape[0]
    slabs = lax.axis_size("slab")
    clip_count, width = clip_cache.shape
    dose_count, focus_count = dose_scale.shape[0], focus_term.shape[0]
    odd = (lax.axis_index("panel") % 2).astype(jnp.int32)

    table_b, ids, own_ids, pairs = layout(
        odd.reshape(1), clip_cache, dose_scale, focus_term, clip_ids, dose_ids, focus_ids
    )
    table_a = from_previous_pair(table_b)
    others = from_other_slabs(own_ids)
    table_d = from_partner(table_b)
    sizes = (clip_count, dose_count, focus_count)
    *counts, table_b = first_counts_of(table_b, own_ids, *sizes)
    table_d, others = lax.optimization_barrier((table_d, others))
    counts = counts_of(others, counts, *sizes)
    more = [from_partner(part) for part in counts]
    table_a, more = lax.optimization_barrier((table_a, more))
    table_c = from_partner(table_a)
    pair_gram = pair_gram_of(counts, more, [table_b, table_d], sizes)
    table_c, pair_gram = lax.optimization_barrier((table_c, pair_gram))
    tables = [table_a, table_b, table_d, table_c]
    own_gram, sent, high, low, doses = quad_gram_of(counts, more, tables, pair_gram, sizes)
    other_gram = from_partner(sent)
    weights = weights_of(odd.reshape(1), pair_gram, own_gram, other_gram, row_count * slabs)
    return rotate(high, low, doses, weights, pairs, ids, tables, sizes)


def solution(mesh):
    return jax.shard_map(
        shards,
        mesh=mesh,
        in_specs=(
            P(None, "panel"),
            P(None, "panel"),
            P(None, "panel"),
            P("slab"),
            P("slab"),
            P("slab"),
        ),
        out_specs=P("slab", "panel"),
        check_vma=False,
    )
```

```python
import jax
import jax.numpy as jnp
from jax import lax
from jax.experimental import pallas as pl
from jax.experimental.pallas import tpu as pltpu
from jax.sharding import PartitionSpec as P

EPSILON = 1e-06
VMEM_LIMIT = 48 * 2**20
HIGHEST = lax.Precision.HIGHEST
COUNT_PARTS = 2
MARGIN = 8
BRIEF = pl.CostEstimate(flops=1, bytes_accessed=1, transcendentals=0)


def from_partner(value):
    count = lax.axis_size("panel")
    return lax.ppermute(value, "panel", [(i, i ^ 1) for i in range(count)])


def from_previous_pair(value):
    count = lax.axis_size("panel")
    return lax.ppermute(value, "panel", [(i, (i + 2) % count) for i in range(count)])


def from_other_slabs(value):
    slabs = lax.axis_size("slab")
    paired = slabs & (slabs - 1) == 0
    target = lambda i, d: i ^ d if paired else (i + d) % slabs
    return [
        lax.ppermute(value, "slab", [(i, target(i, d)) for i in range(slabs)])
        for d in range(1, slabs)
    ]


def split(value):
    high = value.astype(jnp.bfloat16)
    low = (value - high.astype(jnp.float32)).astype(jnp.bfloat16)
    return high, low


def bdot(left, right, dims=((1,), (0,))):
    return lax.dot_general(left, right, (dims, ((), ())), preferred_element_type=jnp.float32)


def split3(value):
    high, rest = split(value)
    middle = value - high.astype(jnp.float32)
    low = (middle - rest.astype(jnp.float32)).astype(jnp.bfloat16)
    return high, rest, low


def dot3(left, right):
    (a, b), (c, d) = split(left), split(right)
    return bdot(jnp.concatenate([a, b, a], axis=1), jnp.concatenate([c, c, d], axis=0))


def dot6(left, right):
    (a, b, c), (d, e, f) = split3(left), split3(right)
    lefts, rights = [a, a, b, b, a, c], [d, e, d, e, f, d]
    return bdot(jnp.concatenate(lefts, axis=1), jnp.concatenate(rights, axis=0))


def dot6_rows(left, right):
    (a, b, c), (d, e, f) = split3(left), split3(right)
    lefts, rights = [a, a, b, b, a, c], [d, e, d, e, f, d]
    return bdot(jnp.concatenate(lefts, axis=1), jnp.concatenate(rights, axis=1), ((1,), (1,)))


def fdot(left, right, dims=((1,), (0,))):
    return lax.dot_general(
        left, right, (dims, ((), ())), precision=HIGHEST, preferred_element_type=jnp.float32
    )


def layout_kernel(odd_ref, clips, doses, focuses, *refs):
    id_refs, outs, spaces, held, sems = refs[:3], refs[3:7], refs[7:10], refs[10:14], refs[14]
    joined, ids, own, pairs = held
    start = 0
    table_copies = []
    for k, ref in enumerate((clips, doses, focuses)):
        part = joined.at[pl.ds(start, ref.shape[0])]
        table_copies.append(pltpu.make_async_copy(ref, part, sems.at[k]))
        start += ref.shape[0]
    id_copies = [
        pltpu.make_async_copy(ref, space, sems.at[3 + k])
        for k, (ref, space) in enumerate(zip(id_refs, spaces))
    ]
    last_copies = [
        pltpu.make_async_copy(value, out, sems.at[6 + k])
        for k, (value, out) in enumerate(zip(held, outs))
    ]
    for copy in table_copies + id_copies:
        copy.start()
    half = own.shape[1]
    begin = pl.multiple_of(odd_ref[0] * half, half)
    for k, (copy, space) in enumerate(zip(id_copies, spaces)):
        copy.wait()
        ids[k : k + 1, :] = space[...]
        own[k : k + 1, :] = space[:, pl.ds(begin, half)]
    sublane = lax.broadcasted_iota(jnp.int32, pairs.shape, 1) & (MARGIN - 1)
    pairs[...] = ids[1:2, :] * clips.shape[0] + ids[0:1, :] + (MARGIN - sublane)
    for copy in table_copies:
        copy.wait()
    for copy in last_copies:
        copy.start()
    for copy in last_copies:
        copy.wait()


def layout(odd, clip_cache, dose_scale, focus_term, *ids):
    rows = clip_cache.shape[0] + dose_scale.shape[0] + focus_term.shape[0]
    count = ids[0].shape[0]
    return pl.pallas_call(
        layout_kernel,
        in_specs=[pl.BlockSpec(memory_space=pltpu.SMEM)]
        + [pl.BlockSpec(memory_space=pltpu.HBM)] * 6,
        out_shape=(
            jax.ShapeDtypeStruct((rows, clip_cache.shape[1]), jnp.float32),
            jax.ShapeDtypeStruct((len(ids), count), jnp.int32),
            jax.ShapeDtypeStruct((len(ids), count // 2), jnp.int32),
            jax.ShapeDtypeStruct((1, count), jnp.int32),
        ),
        out_specs=(pl.BlockSpec(memory_space=pltpu.HBM),) * 4,
        scratch_shapes=[pltpu.VMEM((1, count), jnp.int32)] * 3
        + [pltpu.VMEM((rows, clip_cache.shape[1]), jnp.float32)]
        + [pltpu.VMEM((len(ids), count), jnp.int32), pltpu.VMEM((len(ids), count // 2), jnp.int32)]
        + [pltpu.VMEM((1, count), jnp.int32)]
        + [pltpu.SemaphoreType.DMA((10,))],
        compiler_params=pltpu.CompilerParams(vmem_limit_bytes=60 * 2**20),
        cost_estimate=BRIEF,
        name="layout",
    )(odd, clip_cache, dose_scale, focus_term, *[value.reshape(1, count) for value in ids])


def one_hot(index, first, size):
    positions = first + lax.broadcasted_iota(jnp.int32, (size, index.shape[1]), 0)
    return jnp.where(positions == index, 1.0, 0.0).astype(jnp.bfloat16)


def first_counts_kernel(focus_count, table, ids, *refs):
    outs, copied, sem = refs[:COUNT_PARTS], refs[COUNT_PARTS], refs[COUNT_PARTS + 1]
    copy = pltpu.make_async_copy(table, copied, sem)
    copy.start()
    counts_kernel(focus_count, 0, ids, *outs)
    copy.wait()


def first_counts_of(table, ids, clip_count, dose_count, focus_count):
    settings = dose_count * focus_count
    part = jax.ShapeDtypeStruct((settings // COUNT_PARTS, clip_count), jnp.float32)
    return pl.pallas_call(
        lambda *refs: first_counts_kernel(focus_count, *refs),
        in_specs=[pl.BlockSpec(memory_space=pltpu.HBM), pl.BlockSpec(memory_space=pltpu.VMEM)],
        out_shape=[part] * COUNT_PARTS + [jax.ShapeDtypeStruct(table.shape, table.dtype)],
        scratch_shapes=[pltpu.SemaphoreType.DMA],
        compiler_params=pltpu.CompilerParams(vmem_limit_bytes=VMEM_LIMIT),
        cost_estimate=BRIEF,
        name="counts",
    )(table, ids)


def counts_kernel(focus_count, given, *refs):
    count_refs, id_refs, outs = refs[:given], refs[given : -COUNT_PARTS], refs[-COUNT_PARTS:]
    part, clip_count = outs[0].shape
    settings = part * COUNT_PARTS
    half = clip_count // 2
    chunk = min(2048, id_refs[-1].shape[1])
    total = jnp.zeros((2 * settings, half), jnp.float32)
    for ids in id_refs:
        for start in range(0, ids.shape[1], chunk):
            some = slice(start, start + chunk)
            clip = ids[0:1, some]
            setting = ids[1:2, some] * focus_count + ids[2:3, some]
            upper = clip >= half
            left = one_hot(jnp.where(upper, setting + settings, setting), 0, 2 * settings)
            right = one_hot(jnp.where(upper, clip - half, clip), 0, half)
            total += bdot(left, right, ((1,), (1,)))
    for k, out in enumerate(outs):
        lower = total[k * part : (k + 1) * part]
        upper = total[settings + k * part : settings + (k + 1) * part]
        value = jnp.concatenate([lower, upper], axis=1)
        out[...] = count_refs[k][...] + value if given else value


def counts_of(ids, base, clip_count, dose_count, focus_count):
    settings = dose_count * focus_count
    part = jax.ShapeDtypeStruct((settings // COUNT_PARTS, clip_count), jnp.float32)
    return pl.pallas_call(
        lambda *refs: counts_kernel(focus_count, len(base), *refs),
        out_shape=[part] * COUNT_PARTS,
        compiler_params=pltpu.CompilerParams(vmem_limit_bytes=VMEM_LIMIT),
        cost_estimate=BRIEF,
        name="counts",
    )(*base, *ids)


def prepare_gram(counts, tables, sizes, out, high, low, doses, numbers):
    clip_count, dose_count, focus_count = sizes
    width = out.shape[0]
    panels = len(tables)
    for q, table in enumerate(tables):
        part = slice(q * width, (q + 1) * width)
        high[:, part], low[:, part] = split(table[:clip_count, :])
        doses[:, part] = table[clip_count : clip_count + dose_count, :]
    focuses = jnp.concatenate([table[clip_count + dose_count :, :] for table in tables], axis=1)

    counts_high, counts_low = split(counts)
    totals = (
        bdot(counts_high, high[...]) + bdot(counts_high, low[...]) + bdot(counts_low, high[...])
    )
    mixed = jnp.zeros((focus_count, panels * width), jnp.float32)
    per_focus = jnp.sum(counts, axis=1, keepdims=True)
    number = jnp.zeros((focus_count, 1), jnp.float32)
    for b in range(dose_count):
        some = slice(b * focus_count, (b + 1) * focus_count)
        mixed += totals[some] * doses[b : b + 1, :]
        number += per_focus[some]
        numbers[b : b + 1, :] = jnp.sum(counts[some], axis=0, keepdims=True)
    lefts = jnp.concatenate([focuses[:, :width], mixed[:, :width]], axis=0)
    rights = jnp.concatenate([mixed + number * focuses, focuses], axis=0)
    out[...] = fdot(lefts, rights, ((0,), (0,)))


def add_doses(first, own_doses, begin, group, columns, out, high, low, doses, numbers):
    width = out.shape[0]
    pieces = [first * numbers[pl.ds(begin + k, 1), :] for k in range(group)]
    left_high, left_low = split(jnp.concatenate(pieces, axis=0))
    products = (
        bdot(left_high, high[:, columns])
        + bdot(left_high, low[:, columns])
        + bdot(left_low, high[:, columns])
    )
    lanes = lax.broadcasted_iota(jnp.int32, own_doses.shape, 1)
    total = jnp.zeros_like(out[:, columns])
    for k in range(group):
        column = jnp.sum(jnp.where(lanes == begin + k, own_doses, 0.0), axis=1, keepdims=True)
        row = doses[pl.ds(begin + k, 1), columns]
        total += products[k * width : (k + 1) * width] * column * row
    out[:, columns] += total


def gram_scratch(clip_count, dose_count, total):
    return [
        pltpu.VMEM((clip_count, total), jnp.bfloat16),
        pltpu.VMEM((clip_count, total), jnp.bfloat16),
        pltpu.VMEM((dose_count, total), jnp.float32),
        pltpu.VMEM((dose_count, clip_count), jnp.float32),
    ]


def counts_from(refs):
    own, more = refs[:COUNT_PARTS], refs[COUNT_PARTS:]
    return jnp.concatenate([a[...] + b[...] for a, b in zip(own, more)], axis=0)


def pair_kernel(sizes, *refs):
    counts, refs = refs[: 2 * COUNT_PARTS], refs[2 * COUNT_PARTS :]
    own, partner, out, scratch = refs[0], refs[1], refs[2], refs[3:]
    clip_count, dose_count, _ = sizes
    prepare_gram(counts_from(counts), [own, partner], sizes, out, *scratch)
    first = own[:clip_count, :].T
    own_doses = own[clip_count : clip_count + dose_count, :].T
    group = 8

    def some_doses(step, carry):
        add_doses(first, own_doses, step * group, group, slice(None), out, *scratch)
        return carry

    lax.fori_loop(0, dose_count // group, some_doses, 0)


def pair_gram_of(counts, more, tables, sizes):
    width = tables[0].shape[1]
    return pl.pallas_call(
        lambda *refs: pair_kernel(sizes, *refs),
        out_shape=jax.ShapeDtypeStruct((width, 2 * width), jnp.float32),
        scratch_shapes=gram_scratch(*sizes[:2], 2 * width),
        compiler_params=pltpu.CompilerParams(vmem_limit_bytes=VMEM_LIMIT),
        cost_estimate=BRIEF,
        name="pair_gram",
    )(*counts, *more, *tables)


def quad_kernel(sizes, *refs):
    counts, refs = refs[: 2 * COUNT_PARTS], refs[2 * COUNT_PARTS :]
    tables, earlier, (out, sent, *laid_out) = refs[:4], refs[4], refs[5:]
    clip_count, dose_count, _ = sizes
    width = out.shape[0]
    prepare_gram(counts_from(counts), tables, sizes, out, *laid_out)
    first = tables[0][:clip_count, :].T
    own_doses = tables[0][clip_count : clip_count + dose_count, :].T
    group = 8

    def some_doses(step, carry):
        add_doses(first, own_doses, step * group, group, slice(None), out, *laid_out)
        return carry

    lax.fori_loop(0, dose_count // group, some_doses, 0)
    sent[:, :width] = earlier[:, :width]
    sent[:, width:] = out[:, : 3 * width]


def quad_gram_of(counts, more, tables, earlier, sizes):
    width = tables[0].shape[1]
    clip_count, dose_count, _ = sizes
    square = jax.ShapeDtypeStruct((width, 4 * width), jnp.float32)
    half = jax.ShapeDtypeStruct((clip_count, 4 * width), jnp.bfloat16)
    doses = jax.ShapeDtypeStruct((dose_count, 4 * width), jnp.float32)
    return pl.pallas_call(
        lambda *refs: quad_kernel(sizes, *refs),
        out_shape=(square, square, half, half, doses),
        scratch_shapes=gram_scratch(clip_count, dose_count, 4 * width)[3:],
        compiler_params=pltpu.CompilerParams(vmem_limit_bytes=VMEM_LIMIT),
        cost_estimate=BRIEF,
        name="quad_gram",
    )(*counts, *more, *tables, earlier)


def eye(size):
    rows = lax.broadcasted_iota(jnp.int32, (size, size), 0)
    cols = lax.broadcasted_iota(jnp.int32, (size, size), 1)
    return rows == cols


def diagonal_row(square):
    return jnp.sum(jnp.where(eye(square.shape[0]), square, 0.0), axis=0, keepdims=True)


def column_of(row):
    square = jnp.broadcast_to(row, (row.shape[1], row.shape[1]))
    return jnp.sum(jnp.where(eye(row.shape[1]), square, 0.0), axis=1, keepdims=True)


def inverses(couplings, factors, powers):
    products = [dot6_rows(k, k) for k in couplings]
    bound = jnp.zeros((1, 1), jnp.float32)
    for product in products:
        sums = jnp.sum(jnp.abs(product), axis=0, keepdims=True)
        squares = jnp.sum(product * product, axis=0, keepdims=True)
        frobenius = jnp.sqrt(jnp.sum(squares, axis=1, keepdims=True))
        bound = jnp.maximum(bound, jnp.minimum(jnp.max(sums, axis=1, keepdims=True), frobenius))
    size = products[0].shape[0]
    identity = jnp.where(eye(size), 1.0, 0.0)
    matrices = [identity + product for product in products]
    start = 2.0 / (2.0 + bound)
    for factor, power, matrix in zip(factors, powers, matrices):
        error = identity - start * matrix
        factor[...] = identity + error
        power[...] = dot3(error, error)

    def square(rate):
        for factor, power in zip(factors, powers):
            value, now = power[...], factor[...]
            both = dot3(jnp.concatenate([now, value], axis=0), value)
            factor[...] = now + both[:size]
            power[...] = both[size:]
        return rate * rate

    number = jnp.max(bound)
    rate = number / (2.0 + number)
    lax.while_loop(lambda rate: rate > 3e-4, square, rate * rate)
    for factor in factors:
        factor[...] = start * factor[...]

    def corrected(factor, matrix):
        guess = factor[...]
        return guess + dot3(guess, identity - dot6(matrix, guess))

    def correct(step, carry):
        for factor, matrix in zip(factors, matrices):
            factor[...] = corrected(factor, matrix)
        return carry

    lax.fori_loop(0, jnp.where(number > 4.0, 3, 0), correct, 0)
    return [corrected(factor, matrix) for factor, matrix in zip(factors, matrices)]


def weights_kernel(total_rows, odd_ref, pair_ref, own_ref, other_ref, weights, *spaces):
    width = weights.shape[0]
    odd = odd_ref[0] == 1
    sign = jnp.where(odd, -1.0, 1.0).astype(jnp.float32)
    block = lambda ref, j: ref[:, j * width : (j + 1) * width]
    identity = jnp.where(eye(width), 1.0, 0.0)

    diagonals = [
        diagonal_row(block(own_ref, 0)),
        diagonal_row(block(pair_ref, 0)),
        diagonal_row(block(other_ref, 1)),
        diagonal_row(block(other_ref, 0)),
    ]
    scales = [1.0 / jnp.sqrt(d / total_rows + EPSILON) for d in diagonals]
    columns = [column_of(s) for s in scales]
    scaled = lambda value, i, j: value * columns[i] * scales[j]
    squares = [d * s * s for d, s in zip(diagonals, scales)]

    own_a = scaled(block(own_ref, 0), 0, 0)
    own_b = scaled(block(pair_ref, 0), 1, 1)
    other_a = scaled(block(other_ref, 1), 2, 2)
    other_b = scaled(block(other_ref, 0), 3, 3)
    pair_a = scaled(block(own_ref, 3), 0, 2)
    pair_b = scaled(block(pair_ref, 1), 1, 3)
    cross_oo = scaled(block(own_ref, 1), 0, 1)
    cross_op = scaled(block(own_ref, 2), 0, 3)
    cross_po = scaled(block(other_ref, 3), 2, 1)
    cross_pp = scaled(block(other_ref, 2), 2, 3)

    coupling_a = sign * 0.5 * pair_a / (column_of(squares[0]) + squares[2])
    coupling_b = sign * 0.5 * pair_b / (column_of(squares[1]) + squares[3])
    inverse_a, inverse_b = inverses([coupling_a, coupling_b], spaces[:2], spaces[2:])

    def halves(inverse, coupling):
        own_partner = 2.0 * dot6(inverse, coupling)
        first = (2.0 * inverse - identity, -own_partner.T)
        second = (own_partner, identity - dot3(coupling.T, own_partner))
        return first, second

    own_cols_a, other_cols_a = halves(inverse_a, coupling_a)
    own_cols_b, other_cols_b = halves(inverse_b, coupling_b)
    left = [jnp.where(odd, o, p) for o, p in zip(own_cols_a, other_cols_a)]
    right = [jnp.where(odd, p, o) for o, p in zip(own_cols_b, other_cols_b)]
    left = jnp.concatenate(left, axis=0)
    right = jnp.concatenate(right, axis=0)

    def square_of(a, b, c):
        top = jnp.concatenate([a, b], axis=1)
        return jnp.concatenate([top, jnp.concatenate([b.T, c], axis=1)], axis=0)

    gram_a = square_of(own_a, pair_a, other_a)
    gram_b = square_of(own_b, pair_b, other_b)
    cross = jnp.concatenate(
        [
            jnp.concatenate([cross_oo, cross_op], axis=1),
            jnp.concatenate([cross_po, cross_pp], axis=1),
        ],
        axis=0,
    )
    left_squares = jnp.sum(left * dot3(gram_a, left), axis=0, keepdims=True)
    right_squares = jnp.sum(right * dot3(gram_b, right), axis=0, keepdims=True)
    between = dot3(left.T, dot3(cross, right))
    coupling = 0.5 * between / (column_of(left_squares) + right_squares)
    (inverse,) = inverses([coupling], spaces[:1], spaces[2:3])
    first, second = halves(inverse, coupling)
    top = jnp.where(odd, second[0], first[0])
    bottom = jnp.where(odd, second[1], first[1])
    part_a = dot3(left, top)
    part_b = dot3(right, bottom)
    for k, (part, half, column) in enumerate(
        [(part_a, 0, 0), (part_b, 0, 1), (part_b, 1, 3), (part_a, 1, 2)]
    ):
        piece = part[half * width : (half + 1) * width] * columns[column]
        weights[:, k * width : (k + 1) * width] = piece.T


def weights_of(odd, pair_gram, own_gram, other_gram, total_rows):
    width = own_gram.shape[0]
    whole = lambda value: pl.BlockSpec(value.shape, lambda: (0, 0))
    return pl.pallas_call(
        lambda *refs: weights_kernel(total_rows, *refs),
        in_specs=[pl.BlockSpec(memory_space=pltpu.SMEM)]
        + [whole(value) for value in (pair_gram, own_gram, other_gram)],
        out_specs=pl.BlockSpec((width, 4 * width), lambda: (0, 0)),
        out_shape=jax.ShapeDtypeStruct((width, 4 * width), jnp.float32),
        scratch_shapes=[pltpu.VMEM((width, width), jnp.float32)] * 4,
        compiler_params=pltpu.CompilerParams(vmem_limit_bytes=VMEM_LIMIT),
        name="weights",
    )(odd, pair_gram, own_gram, other_gram)


def rotate_kernel(group, piece, start, high, low, doses, weights, pairs, ids, *refs):
    tables, (out, products, left, places, rows, place_sem, out_sems) = refs[:4], refs[4:]
    clip_count, width = high.shape[0], weights.shape[0]
    over_lanes = ((1,), (1,))
    tall = MARGIN
    fetch = pltpu.make_async_copy(pairs, places, place_sem)
    fetch.start()
    focuses = jnp.concatenate([table[start:, :] for table in tables], axis=1)
    focus_count = focuses.shape[0]
    shifts = jnp.concatenate(split(fdot(focuses, weights[...], over_lanes)), axis=0)
    left[...] = jnp.concatenate([high[...], low[...], high[...]], axis=1)

    def some_doses(step, carry):
        scaled = [weights[...] * doses[pl.ds(step * group + k, 1), :] for k in range(group)]
        right_high, right_low = split(jnp.concatenate(scaled, axis=0))
        right = jnp.concatenate([right_high, right_high, right_low], axis=1)
        result = bdot(left[...], right, over_lanes)
        for k in range(group):
            begin = pl.multiple_of((step * group + k) * clip_count + tall, tall)
            products[pl.ds(begin, clip_count), :] = result[:, k * width : (k + 1) * width]
        return carry

    lax.fori_loop(0, doses.shape[0] // group, some_doses, 0)
    fetch.wait()
    unroll = 512
    sublanes = lax.broadcasted_iota(jnp.int32, (tall, width), 0)
    slots = lax.broadcasted_iota(jnp.int32, (2 * focus_count, piece), 0)
    slots = jnp.where(slots >= focus_count, slots - focus_count, slots)

    def some_rows(part, carry):
        first = pl.multiple_of(part * unroll, unroll)
        for batch in range(0, unroll, 16 * tall):
            tiles = []
            for begin in range(batch, batch + 16 * tall, tall):
                starts = [places[0, first + begin + k] for k in range(tall)]
                found = [products[pl.ds(start, tall), :] for start in starts]
                tile = found[0]
                for k in range(1, tall):
                    tile = jnp.where(sublanes == k, found[k], tile)
                tiles.append((pl.ds(pl.multiple_of(first + begin, tall), tall), tile))
            for where, tile in tiles:
                rows[where, :] += tile
        return carry

    def focus_part(part, carry):
        span = pl.ds(pl.multiple_of(part * piece, piece), piece)
        hot = jnp.where(slots == ids[2:3, span], 1.0, 0.0).astype(jnp.bfloat16)
        rows[span, :] = bdot(hot, shifts, ((0,), (0,)))
        return carry

    lax.fori_loop(0, rows.shape[0] // piece, focus_part, 0)
    copies = []
    for k in range(rows.shape[0] // piece):
        lax.fori_loop(k * piece // unroll, (k + 1) * piece // unroll, some_rows, 0)
        span = pl.ds(k * piece, piece)
        copies.append(pltpu.make_async_copy(rows.at[span], out.at[span], out_sems.at[k]))
        copies[-1].start()
    for copy in copies:
        copy.wait()


def rotate(high, low, doses, weights, pairs, ids, tables, sizes):
    width = weights.shape[0]
    clip_count, dose_count, _ = sizes
    count = pairs.shape[1]
    piece = min(1024, count)
    vmem = pl.BlockSpec(memory_space=pltpu.VMEM)
    return pl.pallas_call(
        lambda *refs: rotate_kernel(8, piece, clip_count + dose_count, *refs),
        in_specs=[vmem] * 4 + [pl.BlockSpec(memory_space=pl.ANY)] + [vmem] * 5,
        out_specs=pl.BlockSpec(memory_space=pltpu.HBM),
        out_shape=jax.ShapeDtypeStruct((count, width), jnp.float32),
        scratch_shapes=[
            pltpu.VMEM((dose_count * clip_count + 2 * MARGIN, width), jnp.float32),
            pltpu.VMEM((clip_count, 3 * high.shape[1]), jnp.bfloat16),
            pltpu.SMEM((1, count), jnp.int32),
            pltpu.VMEM((count, width), jnp.float32),
            pltpu.SemaphoreType.DMA,
            pltpu.SemaphoreType.DMA((count // piece,)),
        ],
        compiler_params=pltpu.CompilerParams(vmem_limit_bytes=VMEM_LIMIT),
        name="rotate",
    )(high, low, doses, weights, pairs, ids, *tables)


def shards(clip_cache, dose_scale, focus_term, clip_ids, dose_ids, focus_ids):
    row_count = clip_ids.shape[0]
    slabs = lax.axis_size("slab")
    clip_count, width = clip_cache.shape
    dose_count, focus_count = dose_scale.shape[0], focus_term.shape[0]
    odd = (lax.axis_index("panel") % 2).astype(jnp.int32)

    table_b, ids, own_ids, pairs = layout(
        odd.reshape(1), clip_cache, dose_scale, focus_term, clip_ids, dose_ids, focus_ids
    )
    table_a = from_previous_pair(table_b)
    others = from_other_slabs(own_ids)
    table_d = from_partner(table_b)
    sizes = (clip_count, dose_count, focus_count)
    *counts, table_b = first_counts_of(table_b, own_ids, *sizes)
    table_d, others = lax.optimization_barrier((table_d, others))
    counts = counts_of(others, counts, *sizes)
    more = [from_partner(part) for part in counts]
    table_a, more = lax.optimization_barrier((table_a, more))
    table_c = from_partner(table_a)
    pair_gram = pair_gram_of(counts, more, [table_b, table_d], sizes)
    table_c, pair_gram = lax.optimization_barrier((table_c, pair_gram))
    tables = [table_a, table_b, table_d, table_c]
    own_gram, sent, high, low, doses = quad_gram_of(counts, more, tables, pair_gram, sizes)
    other_gram = from_partner(sent)
    weights = weights_of(odd.reshape(1), pair_gram, own_gram, other_gram, row_count * slabs)
    return rotate(high, low, doses, weights, pairs, ids, tables, sizes)


def solution(mesh):
    return jax.shard_map(
        shards,
        mesh=mesh,
        in_specs=(
            P(None, "panel"),
            P(None, "panel"),
            P(None, "panel"),
            P("slab"),
            P("slab"),
            P("slab"),
        ),
        out_specs=P("slab", "panel"),
        check_vma=False,
    )
```
